128 devices in a mesh: dp: 8 (over z_lo, x), tensor: 16 (over z_hi, y, core).
Axes of the slice: x: 4, y: 4, z: 4 (z_hi: 2, z_lo: 2; z = z_hi * 2 + z_lo), core: 2. Of those that a mesh axis runs over, the one named last changes fastest.
Arguments:
- tokens: bfloat16 [2048, 4096], P(('dp', 'tensor')), may hold values from -700 to 700
- gate_up: bfloat16 [4096, 2, 14336], P(None, None, 'tensor'), may hold values from -0.09375 to 0.09375
- down_proj: bfloat16 [14336, 4096], P('tensor'), may hold values from -0.046875 to 0.046875
- norm_gain: float32 [4096], replicated, may hold values from 0.5 to 1.5
- act_history: float32 [1], replicated, may hold values from 3 to 8
- grad_history: float32 [1], replicated, may hold values from 20 to 60
- grad_out: bfloat16 [2048, 4096], P(('dp', 'tensor')), may hold values from -240 to 240
Outputs:
- mlp_out: bfloat16 [2048, 4096], P(('dp', 'tensor'))
- grad_tokens: bfloat16 [2048, 4096], P(('dp', 'tensor'))
- grad_gate_up: bfloat16 [4096, 2, 14336], P('dp', None, 'tensor')
- grad_down: bfloat16 [14336, 4096], P(('tensor', 'dp'))
- grad_gain: float32 [4096], replicated
- peak_act: float32 [1], replicated
- peak_grad: float32 [1], replicated
The draws below stay inside these ranges and needn't reach their ends.
All inputs are finite; a program needn't handle non-finite values.
Results may differ from the reference program's by a relative error of at most 0.02.
Values may be sent and summed in bfloat16 or wider, within the bound.
No kernel may reach another device: no remote copies, remote signals or barrier semaphores. Data moves between devices by JAX's collectives and lax.ppermute only.
A program may use at most 192 MiB of HBM per device.

```python
import math
import jax
import jax.numpy as jnp
from jax import lax

D = 4096
FF = 14336
LEN = 256
SEQS = 8
TOKENS = 2048
N_TENSOR = 16


def position_rise(spread):
    places = jnp.arange(TOKENS)
    inside = (places % LEN).astype(jnp.float32) / LEN
    member = (places // LEN).astype(jnp.float32) / SEQS
    return (1.0 + spread * inside) * (1.0 + spread * member)


def log_scales(key, shape, top):
    return jnp.exp(jax.random.uniform(key, shape, jnp.float32, -math.log(top), math.log(top)))


def draw_tokens(key, part):
    key = jax.random.fold_in(key, 5)
    key_base, key_cols, key_rows, key_chan, key_sign = jax.random.split(key, 5)
    base = jax.random.truncated_normal(key_base, -6.0, 6.0, (TOKENS, D), jnp.float32)
    top = 3.1623
    spread = 2.0
    column_scale = log_scales(key_cols, (1, D), top)
    row_scale = log_scales(key_rows, (TOKENS, 1), top)
    channel = jax.random.randint(key_chan, (TOKENS, 1), 0, D)
    signs = (jax.random.randint(key_sign, (TOKENS, 1), 0, 2) * 2 - 1).astype(jnp.float32)
    height = 10.0 * position_rise(spread)[:, None] * signs
    spikes = jnp.where(jnp.arange(D)[None, :] == channel, height, 0.0)
    return ((base * column_scale + spikes) * row_scale).astype(jnp.bfloat16)


def draw_grad_out(key, part):
    key = jax.random.fold_in(key, 9)
    key_base, key_cols, key_rows = jax.random.split(key, 3)
    base = jax.random.truncated_normal(key_base, -6.0, 6.0, (TOKENS, D), jnp.float32)
    top = 3.1623
    spread = 2.0
    column_scale = log_scales(key_cols, (1, D), top)
    row_scale = log_scales(key_rows, (TOKENS, 1), top)
    rising = position_rise(spread)[:, None] / (1.0 + spread)
    return (base * column_scale * row_scale * rising).astype(jnp.bfloat16)


def block_scale(rng, shape, pieces, smallest, high):
    level, own = 1.0, jax.random.fold_in(rng, 6)
    for axis_at, parts in pieces:
        heights = jnp.exp(jax.random.uniform(jax.random.fold_in(own, axis_at), (parts,), jnp.float32, smallest / len(pieces), high / len(pieces)))
        level = level * jnp.repeat(heights, shape[axis_at] // parts).reshape([-1 if axis == axis_at else 1 for axis in range(len(shape))])
    return level


def bell_draw(stream_key, dims, scale, reach, cuts=(), dtype=jnp.bfloat16):
    drawn = jax.random.normal(stream_key, dims, jnp.float32) * scale
    if len(cuts) > 0:
        drawn = block_scale(stream_key, dims, cuts, -0.22, 0.18) * drawn
    return jnp.clip(drawn, min=-reach, max=reach).astype(dtype)


def setup_inputs(seed: int = 0) -> dict:
    key_of = jax.random.split(jax.random.key(seed), 8)
    tokens = draw_tokens(jax.random.fold_in(key_of[7], 71), 0)
    gate_up = bell_draw(key_of[1], (D, 2, FF), D ** -0.5, 0.09375, ((2, 16),))
    down_proj = bell_draw(key_of[2], (FF, D), FF ** -0.5, 0.046875, ((0, 16),))
    norm_gain = jnp.clip(1.0 + 0.1 * jax.random.normal(key_of[3], (D,), jnp.float32), 0.5, 1.5)
    act_history = jnp.clip(jnp.exp(jax.random.uniform(key_of[4], (1,), jnp.float32, math.log(3.0), math.log(8.0))), 3.0, 8.0)
    grad_history = jnp.clip(jnp.exp(jax.random.uniform(key_of[5], (1,), jnp.float32, math.log(20.0), math.log(60.0))), 20.0, 60.0)
    grad_out = draw_grad_out(jax.random.fold_in(key_of[7], 71), 0)
    return {"tokens": tokens, "gate_up": gate_up, "down_proj": down_proj, "norm_gain": norm_gain, "act_history": act_history, "grad_history": grad_history, "grad_out": grad_out}


PEAK = 448.0
EPSILON = 1e-05

def reference(tokens, gate_up, down_proj, norm_gain, act_history, grad_history, grad_out):
    width = FF // N_TENSOR
    root = 1.0 / jnp.sqrt(jnp.float32(TOKENS))
    act_unit = act_history[0] / PEAK
    grad_unit = grad_history[0] / PEAK
    values = tokens.astype(jnp.float32)
    inverse_rms = lax.rsqrt(lax.optimization_barrier(jnp.mean(values * values, axis=-1, keepdims=True)) + EPSILON)
    unit_rows = values * inverse_rms
    normed = unit_rows * norm_gain
    peak_act = jnp.max(jnp.abs(normed)).reshape(1)
    quantized = jnp.clip(normed * (PEAK / act_history[0]), -PEAK, PEAK).astype(jnp.bfloat16)
    grad_quant = jnp.clip(grad_out.astype(jnp.float32) * (PEAK / grad_history[0]), -PEAK, PEAK).astype(jnp.bfloat16)
    paired = gate_up.astype(jnp.float32).reshape(D, 2 * FF)
    down_full = down_proj.astype(jnp.float32)
    quant_seq = quantized.reshape(SEQS, LEN, D)
    grad_seq = grad_quant.reshape(SEQS, LEN, D)

    def one_sequence(carry, inputs):
        sum_pair, sum_down = carry
        quant_rows, grad_rows = inputs
        quant_full = quant_rows.astype(jnp.float32)
        grad_full = grad_rows.astype(jnp.float32)
        projected = jnp.dot(quant_full, paired, precision=lax.Precision.HIGHEST, preferred_element_type=jnp.float32) * act_unit
        pre_gate = projected[:, :FF]
        pre_up = projected[:, FF:]
        sigmoid_gate = jax.nn.sigmoid(pre_gate)
        silu_gate = pre_gate * sigmoid_gate
        hidden = (silu_gate * pre_up).astype(jnp.bfloat16)
        hidden_full = hidden.astype(jnp.float32)
        blocks = jnp.einsum('ltc,tcd->tld', hidden_full.reshape(LEN, N_TENSOR, width), down_full.reshape(N_TENSOR, width, D), precision=lax.Precision.HIGHEST)
        blocks = lax.optimization_barrier(blocks.astype(jnp.bfloat16)).astype(jnp.float32)
        out_rows = lax.optimization_barrier(jnp.sum(blocks, axis=0)).astype(jnp.bfloat16)
        d_hidden = jnp.dot(grad_full, down_full.T, precision=lax.Precision.HIGHEST, preferred_element_type=jnp.float32) * grad_unit
        d_gate = (d_hidden * pre_up * sigmoid_gate * (1.0 + pre_gate * (1.0 - sigmoid_gate))).astype(jnp.bfloat16)
        d_up = (d_hidden * silu_gate).astype(jnp.bfloat16)
        d_pair = jnp.concatenate([d_gate, d_up], axis=1).astype(jnp.float32)
        d_normed = jnp.dot(d_pair, paired.T, precision=lax.Precision.HIGHEST, preferred_element_type=jnp.float32)
        term_pair = jnp.dot(quant_full.T, d_pair, precision=lax.Precision.HIGHEST, preferred_element_type=jnp.float32) * (act_unit * root)
        term_pair = lax.optimization_barrier(term_pair.astype(jnp.bfloat16)).astype(jnp.float32)
        term_down = jnp.dot(hidden_full.T, grad_full, precision=lax.Precision.HIGHEST, preferred_element_type=jnp.float32) * (grad_unit * root)
        term_down = lax.optimization_barrier(term_down.astype(jnp.bfloat16)).astype(jnp.float32)
        return ((sum_pair + term_pair, sum_down + term_down), (out_rows, d_normed))
    start_carry = (jnp.zeros((D, 2 * FF), jnp.float32), jnp.zeros((FF, D), jnp.float32))
    totals, stacked = lax.scan(one_sequence, start_carry, (quant_seq, grad_seq))
    sum_pair, sum_down = totals
    out_seq, normed_seq = stacked
    mlp_out = out_seq.reshape(TOKENS, D)
    d_normed = normed_seq.reshape(TOKENS, D)
    grad_gain = lax.optimization_barrier(jnp.sum(d_normed * unit_rows, axis=0)) * root
    scaled = d_normed * norm_gain
    grad_tokens = (inverse_rms * (scaled - unit_rows * lax.optimization_barrier(jnp.mean(scaled * unit_rows, axis=-1, keepdims=True)))).astype(jnp.bfloat16)
    grad_gate_up = sum_pair.reshape(D, 2, FF).astype(jnp.bfloat16)
    grad_down = sum_down.astype(jnp.bfloat16)
    peak_grad = jnp.max(jnp.abs(grad_out.astype(jnp.float32))).reshape(1)
    return (mlp_out, grad_tokens, grad_gate_up, grad_down, grad_gain, peak_act, peak_grad)
```

```python
import math

import jax
import jax.numpy as jnp
from jax import lax
from jax.sharding import PartitionSpec as P

PEAK = 448.0
EPSILON = 1e-05
ROWS = (((0,), (0,)), ((), ()))
COLS = (((1,), (1,)), ((), ()))
F32 = jnp.float32
BF16 = jnp.bfloat16

RINGS = [[2 * k + core for k in range(8)] for core in range(2)]
CORE = [(i, i ^ 1) for i in range(16)]
ZPAIR = [(i, i ^ 4) for i in range(8)]


def along_x(step):
    return [(z * 4 + x, z * 4 + (x + step) % 4) for z in range(2) for x in range(4)]


def send_x(block, step):
    return lax.ppermute(block, "dp", along_x(step))


def exchange(parts):
    return lax.all_to_all(parts, "tensor", 0, 0, tiled=True, axis_index_groups=RINGS)


def gather_tensor(block):
    own = exchange(jnp.broadcast_to(block[None], (8,) + block.shape))
    other = lax.ppermute(own, "tensor", CORE)
    return own, other


def gather_x(piece):
    left = send_x(piece, 1)
    right = send_x(piece, -1)
    half = piece.shape[0] // 2
    far_top = send_x(left[:half], 1)
    far_low = send_x(right[half:], -1)
    return jnp.concatenate([piece, left, right, far_top, far_low], axis=0)


def quantize(values, unit):
    return jnp.clip(values * unit, -PEAK, PEAK).astype(BF16)


def shards(tokens, gate_up, down_proj, norm_gain, act_history, grad_history, grad_out):
    own_rows, features = tokens.shape
    width = down_proj.shape[0]
    groups = lax.axis_size("dp")
    lanes = lax.axis_size("tensor")
    root = 1.0 / math.sqrt(own_rows * groups * lanes)
    act_unit = act_history[0] / PEAK
    grad_unit = grad_history[0] / PEAK
    dp = lax.axis_index("dp")
    z_lo = dp // 4
    x = dp % 4
    span = features // 8
    half_rows = own_rows * 8

    tokens_own, tokens_other = gather_tensor(tokens)
    grads_own, grads_other = gather_tensor(grad_out)

    values = tokens.astype(F32)
    inverse_rms = lax.rsqrt(jnp.mean(values * values, axis=-1, keepdims=True) + EPSILON)
    unit_rows = values * inverse_rms
    q_mine = quantize(unit_rows * norm_gain, PEAK / act_history[0])
    g_mine = quantize(grad_out.astype(F32), PEAK / grad_history[0])

    def slices(step):
        to = (x + step) % 4

        def cut(rows, z):
            return lax.dynamic_slice(rows, (0, (z * 4 + to) * span), (own_rows, span))

        q_part = jnp.concatenate([cut(q_mine, z_lo), cut(q_mine, 1 - z_lo)], axis=1)
        g_part = jnp.concatenate([cut(g_mine, 0), cut(g_mine, 1)], axis=1)
        return jnp.stack([q_part, g_part])

    sliced = jnp.stack(
        [slices(0), send_x(slices(1), 1), send_x(slices(-1), -1), send_x(slices(2), 2)]
    )
    slices_own, slices_other = gather_tensor(sliced.reshape(4 * 2 * own_rows, 2 * span))

    def lay(k):
        both = jnp.stack([slices_own, slices_other]).reshape(2, 8, 4, 2, own_rows, 2 * span)
        return both[:, :, :, k].transpose(2, 0, 1, 3, 4).reshape(4 * 2 * half_rows, 2 * span)

    q_slice = lay(0)
    g_slice = lay(1)

    rows = jnp.concatenate(
        [tokens_own.reshape(half_rows, features), tokens_other.reshape(half_rows, features)]
    ).astype(F32)
    unit_all = rows * lax.rsqrt(jnp.mean(rows * rows, axis=-1, keepdims=True) + EPSILON)
    normed = unit_all * norm_gain
    local_act = jnp.max(jnp.abs(normed))
    quantized = quantize(normed, PEAK / act_history[0])
    paired = gate_up.reshape(features, 2 * width)
    projected = jnp.dot(quantized, paired, preferred_element_type=F32) * act_unit
    pre_gate = projected[:, :width]
    pre_up = projected[:, width:]
    sigmoid_gate = jax.nn.sigmoid(pre_gate)
    silu_gate = pre_gate * sigmoid_gate
    hidden = (silu_gate * pre_up).astype(BF16)
    hidden_all = gather_x(hidden)

    out_rows = jnp.concatenate(
        [grads_own.reshape(half_rows, features), grads_other.reshape(half_rows, features)]
    ).astype(F32)
    local_grad = jnp.max(jnp.abs(out_rows))
    grad_rows = quantize(out_rows, PEAK / grad_history[0])
    d_hidden = lax.dot_general(grad_rows, down_proj, COLS, preferred_element_type=F32) * grad_unit
    d_gate = (d_hidden * pre_up * sigmoid_gate * (1.0 + pre_gate * (1.0 - sigmoid_gate))).astype(
        BF16
    )
    d_up = (d_hidden * silu_gate).astype(BF16)
    d_pair = jnp.concatenate([d_gate, d_up], axis=1)
    pair_all = gather_x(d_pair)

    share_out = jnp.dot(hidden, down_proj, preferred_element_type=F32).astype(BF16)
    share_normed = lax.dot_general(d_pair, paired, COLS, preferred_element_type=F32)
    gain_share = jnp.sum(share_normed * unit_all, axis=0).reshape(1, features)
    share_normed = share_normed.astype(BF16)

    def pair_sum(share):
        got = lax.ppermute(share[half_rows:], "tensor", CORE)
        total = share[:half_rows].astype(F32) + got.astype(F32)
        return total.astype(BF16).reshape(8, own_rows, features)

    gain_share = gain_share + lax.ppermute(gain_share, "tensor", CORE)
    gain_high = lax.reduce_precision(gain_share, 8, 7)
    gain_rows = jnp.concatenate([gain_high, gain_share - gain_high]).astype(BF16)
    parts = jnp.concatenate(
        [
            pair_sum(share_out),
            pair_sum(share_normed),
            jnp.broadcast_to(gain_rows[None], (8, 2, features)),
        ],
        axis=1,
    )
    totals = jnp.sum(exchange(parts).astype(F32), axis=0)
    mlp_out = totals[:own_rows].astype(BF16)
    d_normed = totals[own_rows : 2 * own_rows]
    gain_sum = totals[2 * own_rows] + totals[2 * own_rows + 1]

    peaks = jnp.concatenate([jnp.full((64,), local_act), jnp.full((64,), local_grad)])
    small = jnp.concatenate([gain_sum.reshape(-1, 128), peaks.reshape(1, 128)])
    small = lax.all_to_all(
        jnp.broadcast_to(small[None], (groups,) + small.shape), "dp", 0, 0, tiled=True
    )
    grad_gain = jnp.sum(small[:, :-1], axis=0).reshape(features) * root
    peak = jnp.max(small[:, -1], axis=0)

    scaled = d_normed * norm_gain
    grad_tokens = (
        inverse_rms * (scaled - unit_rows * jnp.mean(scaled * unit_rows, axis=-1, keepdims=True))
    ).astype(BF16)

    pair_scale = act_unit * root
    down_scale = grad_unit * root
    down_part = (
        lax.dot_general(hidden_all, g_slice, ROWS, preferred_element_type=F32) * down_scale
    ).astype(BF16)
    hand = width // 2
    sent_down = lax.dynamic_slice(down_part, ((1 - z_lo) * hand, 0), (hand, 2 * span))
    kept_down = lax.dynamic_slice(down_part, (z_lo * hand, 0), (hand, 2 * span))
    got_down = lax.ppermute(sent_down, "dp", ZPAIR)
    sum_down = (kept_down.astype(F32) + got_down.astype(F32)).astype(BF16)
    turned = lax.all_to_all(
        sum_down.reshape(4, hand // 4, 2 * span),
        "dp",
        0,
        0,
        tiled=True,
        axis_index_groups=[[0, 1, 2, 3], [4, 5, 6, 7]],
    )
    grad_down = (
        turned.reshape(4, hand // 4, 2, span).transpose(1, 2, 0, 3).reshape(hand // 4, features)
    )

    def pair_grad(part):
        sent = (
            lax.dot_general(q_slice[:, span:], part, ROWS, preferred_element_type=F32) * pair_scale
        ).astype(BF16)
        got = lax.ppermute(sent, "dp", ZPAIR)
        kept = (
            lax.dot_general(q_slice[:, :span], part, ROWS, preferred_element_type=F32) * pair_scale
        )
        return (kept + got.astype(F32)).astype(BF16)

    grad_gate_up = jnp.stack(
        [pair_grad(pair_all[:, :width]), pair_grad(pair_all[:, width:])], axis=1
    )
    return (
        mlp_out,
        grad_tokens,
        grad_gate_up,
        grad_down,
        grad_gain,
        peak[0].reshape(1),
        peak[64].reshape(1),
    )


def solution(mesh):
    placed = (
        P(("dp", "tensor"), None),
        P(None, None, "tensor"),
        P("tensor", None),
        P(),
        P(),
        P(),
        P(("dp", "tensor"), None),
    )
    return jax.shard_map(
        shards,
        mesh=mesh,
        in_specs=placed,
        out_specs=(
            P(("dp", "tensor"), None),
            P(("dp", "tensor"), None),
            P("dp", None, "tensor"),
            P(("tensor", "dp"), None),
            P(),
            P(),
            P(),
        ),
        check_vma=False,
    )
```

```python
import functools
import math

import jax
import jax.numpy as jnp
from jax import lax
from jax.experimental import pallas as pl
from jax.experimental.pallas import tpu as pltpu
from jax.sharding import PartitionSpec as P

PEAK = 448.0
EPSILON = 1e-05
ROWS = (((0,), (0,)), ((), ()))
COLS = (((1,), (1,)), ((), ()))
F32 = jnp.float32
BF16 = jnp.bfloat16
MIB = 1024 * 1024
SMEM = pltpu.SMEM
VMEM = pltpu.VMEM


def options(mib):
    return pltpu.CompilerParams(
        dimension_semantics=("arbitrary",), vmem_limit_bytes=mib * MIB
    )


def cost(macs, moved):
    return pl.CostEstimate(flops=2 * macs, bytes_accessed=moved, transcendentals=0)


def forward_kernel(
    steps, act_ref, own_ref, other_ref, gain_ref, wg_ref, wu_ref,
    hidden_ref, slope_ref, silu_ref, inverse_ref, peak_ref, q_ref, gate_ref, up_ref,
):
    step = pl.program_id(0)
    group = own_ref.shape[1]
    half = own_ref.shape[0] * group
    depth = wg_ref.shape[0]
    chunk = 2 * group

    def take(source, r, columns):
        block = source[r // group : r // group + 2, :, columns]
        return block.reshape(chunk, block.shape[2])

    def quantized(k, slot):
        scale = PEAK / act_ref[0]
        columns = pl.ds(pl.multiple_of(k * depth, depth), depth)
        gain = gain_ref[:, columns]
        peak = peak_ref[...]
        for source, base in ((own_ref, 0), (other_ref, half)):
            for r in range(0, half, chunk):
                rows = pl.ds(base + r, chunk)
                values = take(source, r, columns).astype(F32)
                normed = (values * inverse_ref[rows, :1]) * gain
                q_ref[slot, rows, :] = jnp.clip(normed * scale, -PEAK, PEAK).astype(BF16)
                size = jnp.abs(normed)
                for c in range(0, depth, 128):
                    peak = jnp.maximum(peak, size[:, c : c + 128])
        peak_ref[...] = peak

    @pl.when(step == 0)
    def _():
        peak_ref[...] = jnp.zeros_like(peak_ref)
        gate_ref[...] = jnp.zeros_like(gate_ref)
        up_ref[...] = jnp.zeros_like(up_ref)
        features = own_ref.shape[2]
        for source, base in ((own_ref, 0), (other_ref, half)):
            for r in range(0, half, chunk):
                total = jnp.zeros((chunk, 128), F32)
                for c in range(0, features, 128):
                    values = take(source, r, pl.ds(c, 128)).astype(F32)
                    total += values * values
                mean = jnp.sum(total, axis=-1, keepdims=True) / features
                inverse_ref[pl.ds(base + r, chunk), :] = jnp.broadcast_to(
                    lax.rsqrt(mean + EPSILON), (chunk, 128)
                )
        quantized(0, 0)

    slot = lax.rem(step, 2)
    block = q_ref[slot]
    gate_ref[...] += jnp.dot(block, wg_ref[...], preferred_element_type=F32)
    up_ref[...] += jnp.dot(block, wu_ref[...], preferred_element_type=F32)

    @pl.when(step < steps - 1)
    def _():
        quantized(step + 1, 1 - slot)

    @pl.when(step == steps - 1)
    def _():
        unit = act_ref[0] / PEAK

        @pl.loop(0, gate_ref.shape[0], step=32)
        def _(r):
            rows = pl.ds(pl.multiple_of(r, 32), 32)
            pre_gate = gate_ref[rows, :] * unit
            pre_up = up_ref[rows, :] * unit
            sigmoid = jax.nn.sigmoid(pre_gate)
            silu = pre_gate * sigmoid
            hidden_ref[rows, :] = (silu * pre_up).astype(BF16)
            silu_ref[rows, :] = silu
            slope_ref[rows, :] = pre_up * sigmoid * (1.0 + pre_gate * (1.0 - sigmoid))


def forward(act_history, own, other, gain, paired, depth=1024):
    half, features = own.shape[0] * own.shape[2], own.shape[3]
    width = paired.shape[1] // 2
    steps = features // depth
    rows = 2 * half
    whole = lambda *shape: pl.BlockSpec(shape, lambda i: (0,) * len(shape))
    token_rows = pl.BlockSpec((8, None, own.shape[2], features), lambda i: (0, 0, 0, 0))
    return pl.pallas_call(
        functools.partial(forward_kernel, steps),
        grid=(steps,),
        in_specs=[
            pl.BlockSpec(memory_space=SMEM),
            token_rows,
            token_rows,
            whole(1, features),
            pl.BlockSpec((depth, width), lambda i: (i, 0)),
            pl.BlockSpec((depth, width), lambda i: (i, 1)),
        ],
        out_specs=[
            whole(rows, width),
            whole(rows, width),
            whole(rows, width),
            whole(rows, 128),
            whole(32, 128),
        ],
        out_shape=[
            jax.ShapeDtypeStruct((rows, width), BF16),
            jax.ShapeDtypeStruct((rows, width), F32),
            jax.ShapeDtypeStruct((rows, width), F32),
            jax.ShapeDtypeStruct((rows, 128), F32),
            jax.ShapeDtypeStruct((32, 128), F32),
        ],
        scratch_shapes=[
            VMEM((2, rows, depth), BF16),
            VMEM((rows, width), F32),
            VMEM((rows, width), F32),
        ],
        compiler_params=options(62),
        cost_estimate=cost(rows * features * width * 2, paired.size * 2),
        name="forward",
    )(act_history, own, other, gain, paired, paired)


def both_rows(own_ref, other_ref):
    groups, rows, depth = own_ref.shape
    own = own_ref[...].reshape(groups * rows, depth)
    return jnp.concatenate([own, other_ref[...].reshape(groups * rows, depth)])


def backward_kernel(
    steps, history_ref, own_ref, other_ref, down_ref, slope_ref, silu_ref,
    gate_ref, up_ref, peak_ref, total_ref,
):
    step = pl.program_id(0)

    @pl.when(step == 0)
    def _():
        total_ref[...] = jnp.zeros_like(total_ref)
        peak_ref[...] = jnp.zeros_like(peak_ref)

    values = both_rows(own_ref, other_ref).astype(F32)
    peak_ref[...] = jnp.maximum(peak_ref[...], jnp.max(jnp.abs(values)))
    block = jnp.clip(values * (PEAK / history_ref[0]), -PEAK, PEAK).astype(BF16)
    total_ref[...] += lax.dot_general(block, down_ref[...], COLS, preferred_element_type=F32)

    @pl.when(step == steps - 1)
    def _():
        d_hidden = total_ref[...] * (history_ref[0] / PEAK)
        gate_ref[...] = (d_hidden * slope_ref[...]).astype(BF16)
        up_ref[...] = (d_hidden * silu_ref[...]).astype(BF16)


def backward(grad_history, own, other, down, slope, silu, depth=1024):
    half, features = own.shape[0] * own.shape[2], own.shape[3]
    strip = pl.BlockSpec((8, None, own.shape[2], depth), lambda i: (0, 1, 0, i))
    width = down.shape[0]
    steps = features // depth
    rows = 2 * half
    whole = lambda *shape: pl.BlockSpec(shape, lambda i: (0,) * len(shape))
    return pl.pallas_call(
        functools.partial(backward_kernel, steps),
        grid=(steps,),
        in_specs=[
            pl.BlockSpec(memory_space=SMEM),
            strip,
            strip,
            pl.BlockSpec((width, depth), lambda i: (0, i)),
            whole(rows, width),
            whole(rows, width),
        ],
        out_specs=[whole(rows, width), whole(rows, width), whole(8, 128)],
        out_shape=[
            jax.ShapeDtypeStruct((rows, width), BF16),
            jax.ShapeDtypeStruct((rows, width), BF16),
            jax.ShapeDtypeStruct((8, 128), F32),
        ],
        scratch_shapes=[VMEM((rows, width), F32)],
        compiler_params=options(62),
        cost_estimate=cost(rows * features * width, down.size * 2),
        name="backward",
    )(grad_history, own, other, down, slope, silu)


def out_kernel(hidden_ref, down_ref, own_ref, other_ref):
    half = own_ref.shape[0]
    share = jnp.dot(hidden_ref[...], down_ref[...], preferred_element_type=F32).astype(BF16)
    own_ref[...] = share[:half]
    other_ref[...] = share[half:]


def out_shares(hidden, down, depth=1024):
    rows, width = hidden.shape
    half, features = rows // 2, down.shape[1]
    strip = pl.BlockSpec((half, depth), lambda i: (0, i))
    return pl.pallas_call(
        out_kernel,
        grid=(features // depth,),
        in_specs=[
            pl.BlockSpec((rows, width), lambda i: (0, 0)),
            pl.BlockSpec((width, depth), lambda i: (0, i)),
        ],
        out_specs=[strip, strip],
        out_shape=[jax.ShapeDtypeStruct((half, features), BF16)] * 2,
        compiler_params=options(62),
        cost_estimate=cost(rows * features * width, down.size * 2),
        name="out_shares",
    )(hidden, down)


def normed_kernel(
    gate_ref, up_ref, wg_ref, wu_ref, own_ref, other_ref, inverse_ref,
    norm_own_ref, norm_other_ref, gain_ref,
):
    half = norm_own_ref.shape[0]
    normed = lax.dot_general(gate_ref[...], wg_ref[...], COLS, preferred_element_type=F32)
    normed += lax.dot_general(up_ref[...], wu_ref[...], COLS, preferred_element_type=F32)
    norm_own_ref[...] = normed[:half].astype(BF16)
    norm_other_ref[...] = normed[half:].astype(BF16)
    unit = both_rows(own_ref, other_ref).astype(F32) * inverse_ref[:, :1]
    gain_ref[...] = jnp.sum(normed * unit, axis=0, keepdims=True)


def normed_shares(d_gate, d_up, paired, own, other, inverse, depth=1024):
    half, features = own.shape[0] * own.shape[2], own.shape[3]
    rows, width = d_gate.shape
    token_rows = pl.BlockSpec((8, None, own.shape[2], depth), lambda i: (0, 0, 0, i))
    whole = lambda *shape: pl.BlockSpec(shape, lambda i: (0,) * len(shape))
    strip = pl.BlockSpec((half, depth), lambda i: (0, i))
    return pl.pallas_call(
        normed_kernel,
        grid=(features // depth,),
        in_specs=[
            whole(rows, width),
            whole(rows, width),
            pl.BlockSpec((depth, width), lambda i: (i, 0)),
            pl.BlockSpec((depth, width), lambda i: (i, 1)),
            token_rows,
            token_rows,
            whole(rows, 128),
        ],
        out_specs=[strip, strip, pl.BlockSpec((1, depth), lambda i: (0, i))],
        out_shape=[jax.ShapeDtypeStruct((half, features), BF16)] * 2
        + [jax.ShapeDtypeStruct((1, features), F32)],
        compiler_params=options(62),
        cost_estimate=cost(rows * features * width * 2, paired.size * 2),
        name="normed_shares",
    )(d_gate, d_up, paired, paired, own, other, inverse)


def pack_kernel(out_own, out_got, norm_own, norm_got, parts_ref):
    across = parts_ref.shape[0]
    rows = out_own.shape[0] // (2 * across)
    place = 0
    for own, got in ((out_own, out_got), (norm_own, norm_got)):
        total = (own[...].astype(F32) + got[...].astype(F32)).astype(BF16)
        for h in range(2):
            for y in range(across):
                base = (h * across + y) * rows
                parts_ref[y, place : place + rows] = total[base : base + rows]
            place += rows


def pack(out_own, out_got, norm_own, norm_got, rows, depth=1024):
    half, features = out_own.shape
    strip = pl.BlockSpec((half, depth), lambda i: (0, i))
    total = 4 * rows
    return pl.pallas_call(
        pack_kernel,
        grid=(features // depth,),
        in_specs=[strip] * 4,
        out_specs=pl.BlockSpec((4, total, depth), lambda i: (0, 0, i)),
        out_shape=jax.ShapeDtypeStruct((4, total, features), BF16),
        compiler_params=options(62),
        cost_estimate=cost(2 * half * features, 12 * half * features),
        name="pack",
    )(out_own, out_got, norm_own, norm_got)


def slice_block(own_ref, other_ref):
    parts = []
    for ring in range(4):
        for source in (own_ref, other_ref):
            block = source[:, ring]
            parts.append(block.reshape(block.shape[0] * block.shape[1], block.shape[2]))
    return jnp.concatenate(parts)


def stack_rows(pieces, all_ref):
    rows = pieces[0].shape[0]
    for ring, piece in enumerate(pieces):
        all_ref[ring * rows : (ring + 1) * rows, :] = piece[...]


def pair_kernel(at_ref, scale_ref, p0, p1, p2, p3, own_ref, other_ref, out_ref, all_ref):
    @pl.when(pl.program_id(0) == 0)
    def _():
        stack_rows((p0, p1, p2, p3), all_ref)

    block = slice_block(own_ref, other_ref)
    total = lax.dot_general(block, all_ref[...], ROWS, preferred_element_type=F32)
    out_ref[...] = (total * scale_ref[0]).astype(BF16)


def down_kernel(at_ref, scale_ref, p0, p1, p2, p3, own_ref, other_ref, out_ref, all_ref):
    @pl.when(pl.program_id(0) == 0)
    def _():
        stack_rows((p0, p1, p2, p3), all_ref)

    block = slice_block(own_ref, other_ref)
    total = lax.dot_general(all_ref[...], block, ROWS, preferred_element_type=F32)
    out_ref[...] = (total * scale_ref[0]).astype(BF16)


def contract(kernel, scale, pieces, own, other, first, count, depth=256):
    rows, width = pieces[0].shape
    piece = pl.BlockSpec((rows, width), lambda i, at: (0, 0))
    steps = count // depth
    block = (own.shape[0], 4, own.shape[2], depth)
    cut = pl.BlockSpec(block, lambda i, at: (0, 0, 0, at[0] * steps + i))
    if kernel is pair_kernel:
        shape, spec = (count, width), pl.BlockSpec((depth, width), lambda i, at: (i, 0))
    else:
        shape, spec = (width, count), pl.BlockSpec((width, depth), lambda i, at: (0, i))
    return pl.pallas_call(
        kernel,
        grid_spec=pltpu.PrefetchScalarGridSpec(
            num_scalar_prefetch=1,
            grid=(steps,),
            in_specs=[pl.BlockSpec(memory_space=SMEM)] + [piece] * 4 + [cut, cut],
            out_specs=spec,
            scratch_shapes=[VMEM((4 * rows, width), BF16)],
        ),
        out_shape=jax.ShapeDtypeStruct(shape, BF16),
        compiler_params=options(62),
        cost_estimate=cost(4 * rows * width * count, 8 * rows * (width + count)),
        name="contract_" + ("pair" if kernel is pair_kernel else "down"),
    )(first.reshape(1).astype(jnp.int32), scale, *pieces, own, other)


def join_kernel(g0, g1, u0, u1, out_ref):
    out_ref[:, 0, :] = (g0[...].astype(F32) + g1[...].astype(F32)).astype(BF16)
    out_ref[:, 1, :] = (u0[...].astype(F32) + u1[...].astype(F32)).astype(BF16)


def join(gate_kept, gate_got, up_kept, up_got, depth=128):
    rows, width = gate_kept.shape
    strip = pl.BlockSpec((depth, width), lambda i: (i, 0))
    return pl.pallas_call(
        join_kernel,
        grid=(rows // depth,),
        in_specs=[strip] * 4,
        out_specs=pl.BlockSpec((depth, 2, width), lambda i: (i, 0, 0)),
        out_shape=jax.ShapeDtypeStruct((rows, 2, width), BF16),
        compiler_params=options(62),
        cost_estimate=cost(rows * width, rows * width * 12),
        name="join",
    )(gate_kept, gate_got, up_kept, up_got)

RINGS = [[2 * k + core for k in range(8)] for core in range(2)]
CORE = [(i, i ^ 1) for i in range(16)]
ZPAIR = [(i, i ^ 4) for i in range(8)]
LINES = [[8 * high + 2 * y + core for y in range(4)] for high in range(2) for core in range(2)]
ZFAR = [(i, i ^ 8) for i in range(16)]


def send_y(block, step):
    ring = [
        (8 * high + 2 * y + core, 8 * high + 2 * ((y + step) % 4) + core)
        for high in range(2)
        for y in range(4)
        for core in range(2)
    ]
    return lax.ppermute(block, "tensor", ring)


def exchange(parts):
    return lax.all_to_all(parts, "tensor", 0, 0, tiled=True, axis_index_groups=RINGS)


def exchange_y(parts):
    return lax.all_to_all(parts, "tensor", 0, 0, tiled=True, axis_index_groups=LINES)


def gather_ring(block):
    return exchange(jnp.broadcast_to(block[None], (8,) + block.shape))


def swap_core(block):
    return lax.ppermute(block, "tensor", CORE)


def send_x(block, step):
    ring = [(z * 4 + x, z * 4 + (x + step) % 4) for z in range(2) for x in range(4)]
    return lax.ppermute(block, "dp", ring)


def quantize(values, unit):
    return jnp.clip(values * unit, -PEAK, PEAK).astype(BF16)


def together(*values):
    return lax.optimization_barrier(values)


def after(value, *others):
    return lax.optimization_barrier((value,) + others)[0]


def shards(tokens, gate_up, down_proj, norm_gain, act_history, grad_history, grad_out):
    own_rows, features = tokens.shape
    width = down_proj.shape[0]
    groups = lax.axis_size("dp")
    lanes = lax.axis_size("tensor")
    root = 1.0 / math.sqrt(own_rows * groups * lanes)
    pair_scale = act_history / PEAK * root
    down_scale = grad_history / PEAK * root
    dp = lax.axis_index("dp")
    z_lo = dp // 4
    x = dp % 4
    z_hi = lax.axis_index("tensor") // 8
    span = features // 8
    half = own_rows * 8

    rows_own = gather_ring(jnp.stack([tokens, grad_out]))
    paired = gate_up.reshape(features, 2 * width)

    values = after(tokens, paired).astype(F32)
    inverse_rms = lax.rsqrt(jnp.mean(values * values, axis=-1, keepdims=True) + EPSILON)
    unit_rows = values * inverse_rms
    q_mine = quantize(unit_rows * norm_gain, PEAK / act_history[0])
    g_mine = quantize(grad_out.astype(F32), PEAK / grad_history[0])

    both = jnp.stack([q_mine, g_mine]).reshape(2 * own_rows, 2, 4, span)

    def columns(step):
        cut = lax.dynamic_slice(both, (0, 0, (x + step) % 4, 0), (2 * own_rows, 2, 1, span))
        return cut.reshape(2 * own_rows, 2 * span)

    sliced = jnp.stack(
        [columns(0), send_x(columns(1), 1), send_x(columns(-1), -1), send_x(columns(2), 2)]
    )
    rows_own = after(rows_own, sliced)
    rows_other = swap_core(rows_own)
    sliced = after(sliced, rows_own).reshape(4, 2, own_rows, 2 * span)

    def gather_slices(kind):
        spread = gather_ring(sliced[:, kind].reshape(4 * own_rows, 2 * span))
        return spread.reshape(8, 4, own_rows, 2 * span)

    g_own = gather_slices(1)

    hidden, slope, silu, inverse, act_peak = forward(
        act_history, rows_own, rows_other, norm_gain.reshape(1, features), paired
    )
    hidden, g_own = together(hidden, g_own)

    g_other = swap_core(g_own)
    hidden_left, hidden_right = send_x(hidden, 1), send_x(hidden, -1)
    d_gate, d_up, grad_peak = backward(grad_history, rows_own, rows_other, down_proj, slope, silu)
    hidden, hidden_left, hidden_right, g_other, d_gate, d_up = together(
        hidden, hidden_left, hidden_right, g_other, d_gate, d_up
    )

    q_own = gather_slices(0)
    hidden_far = send_x(hidden, 2)
    gate_left, gate_right = send_x(d_gate, 1), send_x(d_gate, -1)
    norm_own, norm_other, gain_share = normed_shares(
        d_gate, d_up, paired, rows_own, rows_other, inverse
    )
    hidden, hidden_far, gate_left, gate_right, q_own, norm_own, norm_other, gain_share = together(
        hidden, hidden_far, gate_left, gate_right, q_own, norm_own, norm_other, gain_share
    )
    d_gate, d_up, gain_share = together(d_gate, d_up, gain_share)
    hidden_all = (hidden, hidden_left, hidden_right, hidden_far)

    def merge(first, second):
        total = first[:, :features] + second[:, :features]
        peak = jnp.maximum(first[:, features:], second[:, features:])
        return jnp.concatenate([total, peak], axis=1)

    q_other = swap_core(q_own)
    norm_got = swap_core(norm_other)
    gate_far = send_x(d_gate, 2)
    peaks = jnp.concatenate(
        [jnp.full((1, 64), jnp.max(act_peak)), jnp.full((1, 64), jnp.max(grad_peak))], axis=1
    )
    small = jnp.concatenate([gain_share, peaks], axis=1)
    small = merge(small, swap_core(small))
    small = merge(small, lax.ppermute(small, "dp", ZPAIR))
    down_part = contract(
        down_kernel, down_scale, hidden_all, g_own, g_other, z_lo * 0, 2 * span
    )
    hand = width // 2
    sent_down = lax.dynamic_slice(down_part, ((1 - z_lo) * hand, 0), (hand, 2 * span))
    kept_down = lax.dynamic_slice(down_part, (z_lo * hand, 0), (hand, 2 * span))
    sent_down, gate_far, q_other, norm_got, small, d_up, hidden = together(
        sent_down, gate_far, q_other, norm_got, small, d_up, hidden
    )
    gate_all = (d_gate, gate_left, gate_right, gate_far)

    def pair_part(pieces, place, scale=pair_scale):
        return contract(pair_kernel, scale, pieces, q_own, q_other, place, span)

    got_down = lax.ppermute(sent_down, "dp", ZPAIR)
    up_left, up_right = send_x(d_up, 1), send_x(d_up, -1)
    out_own, out_other = out_shares(hidden, down_proj)
    got_down, up_left, up_right, out_own, out_other, d_up, d_gate, norm_own, norm_got, small = (
        together(
            got_down, up_left, up_right, out_own, out_other, d_up, d_gate, norm_own, norm_got, small
        )
    )
    out_got = swap_core(out_other)
    gate_sent = pair_part((d_gate,) + gate_all[1:], 1 - z_lo)
    gate_sent, out_got, d_up, norm_own, norm_got, small = together(
        gate_sent, out_got, d_up, norm_own, norm_got, small
    )

    gate_got = lax.ppermute(gate_sent, "dp", ZPAIR)
    up_far = send_x(d_up, 2)
    small_far, small_left, small_right = send_x(small, 2), send_x(small, 1), send_x(small, -1)
    parts = pack(out_own, out_got, norm_own, norm_got, own_rows)
    up_far, parts, d_up, small, small_far, small_left, small_right = together(
        up_far, parts, d_up, small, small_far, small_left, small_right
    )
    sums = exchange_y(parts)

    up_all = (d_up, up_left, up_right, up_far)
    up_sent = pair_part(up_all, 1 - z_lo)
    up_sent, small, small_far, small_left, small_right, kept_down, got_down, late_scale = (
        together(
            up_sent, small, small_far, small_left, small_right, kept_down, got_down, pair_scale
        )
    )
    small = merge(merge(small, small_far), merge(small_left, small_right))
    up_got = lax.ppermute(up_sent, "dp", ZPAIR)
    small_far, small_left, small_right = send_y(small, 2), send_y(small, 1), send_y(small, -1)
    gate_kept = pair_part(gate_all, z_lo, late_scale)
    up_kept = pair_part(up_all, z_lo, late_scale)

    sum_down = (kept_down.astype(F32) + got_down.astype(F32)).astype(BF16)
    sum_down = sum_down.reshape(4, hand // 4, 2 * span)

    def own_part(step):
        return lax.dynamic_index_in_dim(sum_down, (x + step) % 4, 0, keepdims=False)

    turned = jnp.stack(
        [own_part(0), send_x(own_part(1), 1), send_x(own_part(2), 2), send_x(own_part(-1), -1)]
    )
    turned = turned[(x - jnp.arange(4)) % 4]
    grad_down = (
        turned.reshape(4, hand // 4, 2, span).transpose(1, 2, 0, 3).reshape(hand // 4, features)
    )

    up_got, gate_kept, up_kept, grad_down, small, small_far, small_left, small_right, sums = together(
        up_got, gate_kept, up_kept, grad_down, small, small_far, small_left, small_right, sums
    )
    small = merge(merge(small, small_far), merge(small_left, small_right))
    totals = jnp.sum(sums.astype(F32), axis=0)
    rows = totals.reshape(2, 2, own_rows, features)
    kept = lax.dynamic_index_in_dim(rows, z_hi, 1, keepdims=False)
    sent = lax.dynamic_index_in_dim(rows, 1 - z_hi, 1, keepdims=False).astype(BF16)
    rows = kept + lax.ppermute(sent, "tensor", ZFAR).astype(F32)
    mlp_out = rows[0].astype(BF16)
    d_normed = rows[1]
    gain_sum = small[0, :features]
    grad_gain = (gain_sum + lax.ppermute(gain_sum, "tensor", ZFAR)) * root
    scaled = d_normed * norm_gain
    grad_tokens = (
        inverse_rms * (scaled - unit_rows * jnp.mean(scaled * unit_rows, axis=-1, keepdims=True))
    ).astype(BF16)
    grad_gate_up = join(gate_kept, gate_got, up_kept, up_got)
    return (
        mlp_out,
        grad_tokens,
        grad_gate_up,
        grad_down,
        grad_gain,
        small[0, features : features + 1],
        small[0, features + 64 : features + 65],
    )


def solution(mesh):
    placed = (
        P(("dp", "tensor"), None),
        P(None, None, "tensor"),
        P("tensor", None),
        P(),
        P(),
        P(),
        P(("dp", "tensor"), None),
    )
    return jax.shard_map(
        shards,
        mesh=mesh,
        in_specs=placed,
        out_specs=(
            P(("dp", "tensor"), None),
            P(("dp", "tensor"), None),
            P("dp", None, "tensor"),
            P(("tensor", "dp"), None),
            P(),
            P(),
            P(),
        ),
        check_vma=False,
    )
```

```python
import functools
import math

import jax
import jax.numpy as jnp
from jax import lax
from jax.experimental import pallas as pl
from jax.experimental.pallas import tpu as pltpu
from jax.sharding import PartitionSpec as P

PEAK = 448.0
EPSILON = 1e-05
ROWS = (((0,), (0,)), ((), ()))
COLS = (((1,), (1,)), ((), ()))
F32 = jnp.float32
BF16 = jnp.bfloat16
MIB = 1024 * 1024
SMEM = pltpu.SMEM
VMEM = pltpu.VMEM


def options(mib):
    return pltpu.CompilerParams(
        dimension_semantics=("arbitrary",), vmem_limit_bytes=mib * MIB
    )


def cost(macs, moved):
    return pl.CostEstimate(flops=2 * macs, bytes_accessed=moved, transcendentals=0)


def forward_kernel(
    steps, act_ref, own_ref, other_ref, gain_ref, wg_ref, wu_ref,
    hidden_ref, slope_ref, silu_ref, inverse_ref, peak_ref, q_ref, gate_ref, up_ref,
):
    step = pl.program_id(0)
    group = own_ref.shape[1]
    half = own_ref.shape[0] * group
    depth = wg_ref.shape[0]
    chunk = 2 * group

    def take(source, r, columns):
        block = source[r // group : r // group + 2, :, columns]
        return block.reshape(chunk, block.shape[2])

    def quantized(k, slot):
        scale = PEAK / act_ref[0]
        columns = pl.ds(pl.multiple_of(k * depth, depth), depth)
        gain = gain_ref[:, columns]
        peak = peak_ref[...]
        for source, base in ((own_ref, 0), (other_ref, half)):
            for r in range(0, half, chunk):
                rows = pl.ds(base + r, chunk)
                values = take(source, r, columns).astype(F32)
                normed = (values * inverse_ref[rows, :1]) * gain
                q_ref[slot, rows, :] = jnp.clip(normed * scale, -PEAK, PEAK).astype(BF16)
                size = jnp.abs(normed)
                for c in range(0, depth, 128):
                    peak = jnp.maximum(peak, size[:, c : c + 128])
        peak_ref[...] = peak

    @pl.when(step == 0)
    def _():
        peak_ref[...] = jnp.zeros_like(peak_ref)
        gate_ref[...] = jnp.zeros_like(gate_ref)
        up_ref[...] = jnp.zeros_like(up_ref)
        features = own_ref.shape[2]
        for source, base in ((own_ref, 0), (other_ref, half)):
            for r in range(0, half, chunk):
                total = jnp.zeros((chunk, 128), F32)
                for c in range(0, features, 128):
                    values = take(source, r, pl.ds(c, 128)).astype(F32)
                    total += values * values
                mean = jnp.sum(total, axis=-1, keepdims=True) / features
                inverse_ref[pl.ds(base + r, chunk), :] = jnp.broadcast_to(
                    lax.rsqrt(mean + EPSILON), (chunk, 128)
                )
        quantized(0, 0)

    slot = lax.rem(step, 2)
    block = q_ref[slot]
    gate_ref[...] += jnp.dot(block, wg_ref[...], preferred_element_type=F32)
    up_ref[...] += jnp.dot(block, wu_ref[...], preferred_element_type=F32)

    @pl.when(step < steps - 1)
    def _():
        quantized(step + 1, 1 - slot)

    @pl.when(step == steps - 1)
    def _():
        unit = act_ref[0] / PEAK

        @pl.loop(0, gate_ref.shape[0], step=32)
        def _(r):
            rows = pl.ds(pl.multiple_of(r, 32), 32)
            pre_gate = gate_ref[rows, :] * unit
            pre_up = up_ref[rows, :] * unit
            sigmoid = jax.nn.sigmoid(pre_gate)
            silu = pre_gate * sigmoid
            hidden_ref[rows, :] = (silu * pre_up).astype(BF16)
            silu_ref[rows, :] = silu
            slope_ref[rows, :] = pre_up * sigmoid * (1.0 + pre_gate * (1.0 - sigmoid))


def forward(act_history, own, other, gain, paired, depth=1024):
    half, features = own.shape[0] * own.shape[2], own.shape[3]
    width = paired.shape[1] // 2
    steps = features // depth
    rows = 2 * half
    whole = lambda *shape: pl.BlockSpec(shape, lambda i: (0,) * len(shape))
    token_rows = pl.BlockSpec((8, None, own.shape[2], features), lambda i: (0, 0, 0, 0))
    return pl.pallas_call(
        functools.partial(forward_kernel, steps),
        grid=(steps,),
        in_specs=[
            pl.BlockSpec(memory_space=SMEM),
            token_rows,
            token_rows,
            whole(1, features),
            pl.BlockSpec((depth, width), lambda i: (i, 0)),
            pl.BlockSpec((depth, width), lambda i: (i, 1)),
        ],
        out_specs=[
            whole(rows, width),
            whole(rows, width),
            whole(rows, width),
            whole(rows, 128),
            whole(32, 128),
        ],
        out_shape=[
            jax.ShapeDtypeStruct((rows, width), BF16),
            jax.ShapeDtypeStruct((rows, width), F32),
            jax.ShapeDtypeStruct((rows, width), F32),
            jax.ShapeDtypeStruct((rows, 128), F32),
            jax.ShapeDtypeStruct((32, 128), F32),
        ],
        scratch_shapes=[
            VMEM((2, rows, depth), BF16),
            VMEM((rows, width), F32),
            VMEM((rows, width), F32),
        ],
        compiler_params=options(62),
        cost_estimate=cost(rows * features * width * 2, paired.size * 2),
        name="forward",
    )(act_history, own, other, gain, paired, paired)


def both_rows(own_ref, other_ref):
    groups, rows, depth = own_ref.shape
    own = own_ref[...].reshape(groups * rows, depth)
    return jnp.concatenate([own, other_ref[...].reshape(groups * rows, depth)])


def backward_kernel(
    steps, history_ref, own_ref, other_ref, down_ref, slope_ref, silu_ref,
    gate_ref, up_ref, peak_ref, total_ref,
):
    step = pl.program_id(0)

    @pl.when(step == 0)
    def _():
        total_ref[...] = jnp.zeros_like(total_ref)
        peak_ref[...] = jnp.zeros_like(peak_ref)

    values = both_rows(own_ref, other_ref).astype(F32)
    peak_ref[...] = jnp.maximum(peak_ref[...], jnp.max(jnp.abs(values)))
    block = jnp.clip(values * (PEAK / history_ref[0]), -PEAK, PEAK).astype(BF16)
    total_ref[...] += lax.dot_general(block, down_ref[...], COLS, preferred_element_type=F32)

    @pl.when(step == steps - 1)
    def _():
        d_hidden = total_ref[...] * (history_ref[0] / PEAK)
        gate_ref[...] = (d_hidden * slope_ref[...]).astype(BF16)
        up_ref[...] = (d_hidden * silu_ref[...]).astype(BF16)


def backward(grad_history, own, other, down, slope, silu, depth=1024):
    half, features = own.shape[0] * own.shape[2], own.shape[3]
    strip = pl.BlockSpec((8, None, own.shape[2], depth), lambda i: (0, 1, 0, i))
    width = down.shape[0]
    steps = features // depth
    rows = 2 * half
    whole = lambda *shape: pl.BlockSpec(shape, lambda i: (0,) * len(shape))
    return pl.pallas_call(
        functools.partial(backward_kernel, steps),
        grid=(steps,),
        in_specs=[
            pl.BlockSpec(memory_space=SMEM),
            strip,
            strip,
            pl.BlockSpec((width, depth), lambda i: (0, i)),
            whole(rows, width),
            whole(rows, width),
        ],
        out_specs=[whole(rows, width), whole(rows, width), whole(8, 128)],
        out_shape=[
            jax.ShapeDtypeStruct((rows, width), BF16),
            jax.ShapeDtypeStruct((rows, width), BF16),
            jax.ShapeDtypeStruct((8, 128), F32),
        ],
        scratch_shapes=[VMEM((rows, width), F32)],
        compiler_params=options(62),
        cost_estimate=cost(rows * features * width, down.size * 2),
        name="backward",
    )(grad_history, own, other, down, slope, silu)


def out_kernel(hidden_ref, down_ref, own_ref, other_ref):
    half = own_ref.shape[0]
    share = jnp.dot(hidden_ref[...], down_ref[...], preferred_element_type=F32).astype(BF16)
    own_ref[...] = share[:half]
    other_ref[...] = share[half:]


def out_shares(hidden, down, depth=1024):
    rows, width = hidden.shape
    half, features = rows // 2, down.shape[1]
    strip = pl.BlockSpec((half, depth), lambda i: (0, i))
    return pl.pallas_call(
        out_kernel,
        grid=(features // depth,),
        in_specs=[
            pl.BlockSpec((rows, width), lambda i: (0, 0)),
            pl.BlockSpec((width, depth), lambda i: (0, i)),
        ],
        out_specs=[strip, strip],
        out_shape=[jax.ShapeDtypeStruct((half, features), BF16)] * 2,
        compiler_params=options(62),
        cost_estimate=cost(rows * features * width // 50, down.size // 25),
        name="out_shares",
    )(hidden, down)


def normed_kernel(
    gate_ref, up_ref, wg_ref, wu_ref, own_ref, other_ref, inverse_ref,
    norm_own_ref, norm_other_ref, gain_ref,
):
    half = norm_own_ref.shape[0]
    normed = lax.dot_general(gate_ref[...], wg_ref[...], COLS, preferred_element_type=F32)
    normed += lax.dot_general(up_ref[...], wu_ref[...], COLS, preferred_element_type=F32)
    norm_own_ref[...] = normed[:half].astype(BF16)
    norm_other_ref[...] = normed[half:].astype(BF16)
    unit = both_rows(own_ref, other_ref).astype(F32) * inverse_ref[:, :1]
    gain_ref[...] = jnp.sum(normed * unit, axis=0, keepdims=True)


def normed_shares(d_gate, d_up, paired, own, other, inverse, depth=1024):
    half, features = own.shape[0] * own.shape[2], own.shape[3]
    rows, width = d_gate.shape
    token_rows = pl.BlockSpec((8, None, own.shape[2], depth), lambda i: (0, 0, 0, i))
    whole = lambda *shape: pl.BlockSpec(shape, lambda i: (0,) * len(shape))
    strip = pl.BlockSpec((half, depth), lambda i: (0, i))
    return pl.pallas_call(
        normed_kernel,
        grid=(features // depth,),
        in_specs=[
            whole(rows, width),
            whole(rows, width),
            pl.BlockSpec((depth, width), lambda i: (i, 0)),
            pl.BlockSpec((depth, width), lambda i: (i, 1)),
            token_rows,
            token_rows,
            whole(rows, 128),
        ],
        out_specs=[strip, strip, pl.BlockSpec((1, depth), lambda i: (0, i))],
        out_shape=[jax.ShapeDtypeStruct((half, features), BF16)] * 2
        + [jax.ShapeDtypeStruct((1, features), F32)],
        compiler_params=options(62),
        cost_estimate=cost(rows * features * width * 2, paired.size * 2),
        name="normed_shares",
    )(d_gate, d_up, paired, paired, own, other, inverse)


def pack_kernel(out_own, out_got, norm_own, norm_got, gain_ref, parts_ref):
    across = parts_ref.shape[0]
    rows = out_own.shape[0] // (2 * across)
    place = 0
    for own, got in ((out_own, out_got), (norm_own, norm_got)):
        total = (own[...].astype(F32) + got[...].astype(F32)).astype(BF16)
        for h in range(2):
            for y in range(across):
                base = (h * across + y) * rows
                parts_ref[y, place : place + rows] = total[base : base + rows]
            place += rows
    gain = gain_ref[...]
    upper = gain.astype(BF16)
    lower = (gain - upper.astype(F32)).astype(BF16)
    both = jnp.concatenate([upper, lower])
    for y in range(across):
        parts_ref[y, place:] = both


def pack(out_own, out_got, norm_own, norm_got, gain, rows, depth=1024):
    half, features = out_own.shape
    strip = pl.BlockSpec((half, depth), lambda i: (0, i))
    total = 4 * rows + 2
    return pl.pallas_call(
        pack_kernel,
        grid=(features // depth,),
        in_specs=[strip] * 4 + [pl.BlockSpec((1, depth), lambda i: (0, i))],
        out_specs=pl.BlockSpec((4, total, depth), lambda i: (0, 0, i)),
        out_shape=jax.ShapeDtypeStruct((4, total, features), BF16),
        compiler_params=options(62),
        cost_estimate=cost(half * features // 25, half * features // 4),
        name="pack",
    )(out_own, out_got, norm_own, norm_got, gain)


def slice_block(own_ref, other_ref):
    parts = []
    for ring in range(4):
        for source in (own_ref, other_ref):
            block = source[:, ring]
            parts.append(block.reshape(block.shape[0] * block.shape[1], block.shape[2]))
    return jnp.concatenate(parts)


def stack_rows(pieces, all_ref):
    rows = pieces[0].shape[0]
    for ring, piece in enumerate(pieces):
        all_ref[ring * rows : (ring + 1) * rows, :] = piece[...]


def pair_kernel(at_ref, scale_ref, p0, p1, p2, p3, own_ref, other_ref, out_ref, all_ref):
    @pl.when(pl.program_id(0) == 0)
    def _():
        stack_rows((p0, p1, p2, p3), all_ref)

    block = slice_block(own_ref, other_ref)
    total = lax.dot_general(block, all_ref[...], ROWS, preferred_element_type=F32)
    out_ref[...] = (total * scale_ref[0]).astype(BF16)


def down_kernel(at_ref, scale_ref, p0, p1, p2, p3, own_ref, other_ref, out_ref, all_ref):
    @pl.when(pl.program_id(0) == 0)
    def _():
        stack_rows((p0, p1, p2, p3), all_ref)

    block = slice_block(own_ref, other_ref)
    total = lax.dot_general(all_ref[...], block, ROWS, preferred_element_type=F32)
    out_ref[...] = (total * scale_ref[0]).astype(BF16)


def contract(kernel, scale, pieces, own, other, kind, first, count, share=1, depth=256):
    rows, width = pieces[0].shape
    piece = pl.BlockSpec((rows, width), lambda i, at: (0, 0))
    steps = count // depth
    block = (own.shape[0], 4, None, own.shape[3], depth)
    cut = pl.BlockSpec(block, lambda i, at: (0, 0, kind, 0, at[0] * steps + i))
    if kernel is pair_kernel:
        shape, spec = (count, width), pl.BlockSpec((depth, width), lambda i, at: (i, 0))
    else:
        shape, spec = (width, count), pl.BlockSpec((width, depth), lambda i, at: (0, i))
    return pl.pallas_call(
        kernel,
        grid_spec=pltpu.PrefetchScalarGridSpec(
            num_scalar_prefetch=1,
            grid=(steps,),
            in_specs=[pl.BlockSpec(memory_space=SMEM)] + [piece] * 4 + [cut, cut],
            out_specs=spec,
            scratch_shapes=[VMEM((4 * rows, width), BF16)],
        ),
        out_shape=jax.ShapeDtypeStruct(shape, BF16),
        compiler_params=options(62),
        cost_estimate=cost(4 * rows * width * count // share, 8 * rows * (width + count) // share),
        name="contract_" + ("pair" if kernel is pair_kernel else "down"),
    )(first.reshape(1).astype(jnp.int32), scale, *pieces, own, other)


def join_kernel(g0, g1, u0, u1, out_ref):
    out_ref[:, 0, :] = (g0[...].astype(F32) + g1[...].astype(F32)).astype(BF16)
    out_ref[:, 1, :] = (u0[...].astype(F32) + u1[...].astype(F32)).astype(BF16)


def join(gate_kept, gate_got, up_kept, up_got, depth=128):
    rows, width = gate_kept.shape
    strip = pl.BlockSpec((depth, width), lambda i: (i, 0))
    return pl.pallas_call(
        join_kernel,
        grid=(rows // depth,),
        in_specs=[strip] * 4,
        out_specs=pl.BlockSpec((depth, 2, width), lambda i: (i, 0, 0)),
        out_shape=jax.ShapeDtypeStruct((rows, 2, width), BF16),
        compiler_params=options(62),
        cost_estimate=cost(rows * width, rows * width * 12),
        name="join",
    )(gate_kept, gate_got, up_kept, up_got)

RINGS = [[2 * k + core for k in range(8)] for core in range(2)]
CORE = [(i, i ^ 1) for i in range(16)]
ZPAIR = [(i, i ^ 4) for i in range(8)]
LINES = [[8 * high + 2 * y + core for y in range(4)] for high in range(2) for core in range(2)]
ZFAR = [(i, i ^ 8) for i in range(16)]


def send_y(block, step):
    ring = [
        (8 * high + 2 * y + core, 8 * high + 2 * ((y + step) % 4) + core)
        for high in range(2)
        for y in range(4)
        for core in range(2)
    ]
    return lax.ppermute(block, "tensor", ring)


def exchange(parts):
    return lax.all_to_all(parts, "tensor", 0, 0, tiled=True, axis_index_groups=RINGS)


def exchange_y(parts):
    return lax.all_to_all(parts, "tensor", 0, 0, tiled=True, axis_index_groups=LINES)


def gather_ring(block):
    return exchange(jnp.broadcast_to(block[None], (8,) + block.shape))


def swap_core(block):
    return lax.ppermute(block, "tensor", CORE)


def send_x(block, step):
    ring = [(z * 4 + x, z * 4 + (x + step) % 4) for z in range(2) for x in range(4)]
    return lax.ppermute(block, "dp", ring)


def quantize(values, unit):
    return jnp.clip(values * unit, -PEAK, PEAK).astype(BF16)


def together(*values):
    return lax.optimization_barrier(values)


def after(value, *others):
    return lax.optimization_barrier((value,) + others)[0]


def shards(tokens, gate_up, down_proj, norm_gain, act_history, grad_history, grad_out):
    own_rows, features = tokens.shape
    width = down_proj.shape[0]
    groups = lax.axis_size("dp")
    lanes = lax.axis_size("tensor")
    root = 1.0 / math.sqrt(own_rows * groups * lanes)
    pair_scale = act_history / PEAK * root
    down_scale = grad_history / PEAK * root
    dp = lax.axis_index("dp")
    z_lo = dp // 4
    x = dp % 4
    z_hi = lax.axis_index("tensor") // 8
    span = features // 8
    half = own_rows * 8

    rows_own = gather_ring(jnp.stack([tokens, grad_out]))
    paired = gate_up.reshape(features, 2 * width)

    values = after(tokens, paired).astype(F32)
    inverse_rms = lax.rsqrt(jnp.mean(values * values, axis=-1, keepdims=True) + EPSILON)
    unit_rows = values * inverse_rms
    q_mine = quantize(unit_rows * norm_gain, PEAK / act_history[0])
    g_mine = quantize(grad_out.astype(F32), PEAK / grad_history[0])

    both = jnp.stack([q_mine, g_mine]).reshape(2 * own_rows, 2, 4, span)

    def columns(step):
        cut = lax.dynamic_slice(both, (0, 0, (x + step) % 4, 0), (2 * own_rows, 2, 1, span))
        return cut.reshape(2 * own_rows, 2 * span)

    sliced = jnp.stack(
        [columns(0), send_x(columns(1), 1), send_x(columns(-1), -1), send_x(columns(2), 2)]
    )
    rows_own = after(rows_own, sliced)
    rows_other = swap_core(rows_own)

    hidden, slope, silu, inverse, act_peak = forward(
        act_history, rows_own, rows_other, norm_gain.reshape(1, features), paired
    )
    hidden, sliced = together(hidden, sliced)

    slices_own = gather_ring(sliced.reshape(8 * own_rows, 2 * span))
    hidden_left, hidden_right = send_x(hidden, 1), send_x(hidden, -1)
    d_gate, d_up, grad_peak = backward(grad_history, rows_own, rows_other, down_proj, slope, silu)
    hidden, hidden_left, hidden_right, d_gate, d_up = together(
        hidden, hidden_left, hidden_right, d_gate, d_up
    )

    hidden_far = send_x(hidden, 2)
    gate_left, gate_right = send_x(d_gate, 1), send_x(d_gate, -1)
    norm_own, norm_other, gain_share = normed_shares(
        d_gate, d_up, paired, rows_own, rows_other, inverse
    )
    out_own, out_other = out_shares(after(hidden, norm_own), down_proj)
    gain_share = gain_share + swap_core(gain_share)
    peaks = jnp.concatenate(
        [jnp.full((1, 64), jnp.max(act_peak)), jnp.full((1, 64), jnp.max(grad_peak))], axis=1
    )
    small = jnp.concatenate([gain_share.reshape(-1, 128), peaks])
    small = jnp.broadcast_to(small[None], (groups,) + small.shape)
    hidden, hidden_far, gate_left, gate_right, norm_own, norm_other, small, d_gate, d_up = together(
        hidden, hidden_far, gate_left, gate_right, norm_own, norm_other, small, d_gate, d_up
    )
    slices_own, norm_other, out_own, out_other = together(
        slices_own, norm_other, out_own, out_other
    )
    slices_own = slices_own.reshape(8, 4, 2, own_rows, 2 * span)
    slices_other = swap_core(slices_own)
    hidden_all = (hidden, hidden_left, hidden_right, hidden_far)

    norm_got = swap_core(norm_other)
    out_got = swap_core(out_other)
    small = lax.all_to_all(small, "dp", 0, 0, tiled=True)
    gate_far = send_x(d_gate, 2)
    down_part = contract(
        down_kernel, down_scale, hidden_all, slices_own, slices_other, 1, z_lo * 0, 2 * span
    )
    hand = width // 2
    sent_down = lax.dynamic_slice(down_part, ((1 - z_lo) * hand, 0), (hand, 2 * span))
    kept_down = lax.dynamic_slice(down_part, (z_lo * hand, 0), (hand, 2 * span))
    sent_down, gate_far, norm_got, out_got, small, d_up = together(
        sent_down, gate_far, norm_got, out_got, small, d_up
    )
    gate_all = (d_gate, gate_left, gate_right, gate_far)

    def pair_part(pieces, place, share=1, scale=pair_scale):
        return contract(
            pair_kernel, scale, pieces, slices_own, slices_other, 0, place, span, share
        )

    got_down = lax.ppermute(sent_down, "dp", ZPAIR)
    up_all = (d_up, send_x(d_up, 1), send_x(d_up, -1), send_x(d_up, 2))
    gate_sent = pair_part(gate_all, 1 - z_lo)
    gain_sum = jnp.sum(small[:, :-1], axis=0).reshape(1, features)
    peak = jnp.max(small[:, -1], axis=0)
    parts = pack(out_own, out_got, norm_own, norm_got, after(gain_sum, gate_sent), own_rows)
    sums = exchange_y(parts)
    got_down, up_all, gate_sent, parts, late_scale = together(
        got_down, up_all, gate_sent, parts, pair_scale
    )

    gate_got = lax.ppermute(gate_sent, "dp", ZPAIR)
    up_sent = pair_part(up_all, 1 - z_lo, 50, late_scale)
    up_got = lax.ppermute(up_sent, "dp", ZPAIR)
    gate_kept = pair_part(gate_all, z_lo, 50, after(late_scale, up_sent))
    up_kept = pair_part(up_all, z_lo, 50, after(late_scale, up_sent))
    gate_got, gate_kept, up_kept, kept_down, got_down = together(
        gate_got, gate_kept, up_kept, kept_down, got_down
    )

    sum_down = (kept_down.astype(F32) + got_down.astype(F32)).astype(BF16)
    sum_down = sum_down.reshape(4, hand // 4, 2 * span)

    def own_part(step):
        return lax.dynamic_index_in_dim(sum_down, (x + step) % 4, 0, keepdims=False)

    turned = jnp.stack(
        [own_part(0), send_x(own_part(1), 1), send_x(own_part(2), 2), send_x(own_part(-1), -1)]
    )
    turned = turned[(x - jnp.arange(4)) % 4]
    grad_down = (
        turned.reshape(4, hand // 4, 2, span).transpose(1, 2, 0, 3).reshape(hand // 4, features)
    )

    gate_got, up_got, gate_kept, up_kept, grad_down, sums = together(
        gate_got, up_got, gate_kept, up_kept, grad_down, sums
    )
    totals = jnp.sum(sums.astype(F32), axis=0)
    rows = totals[: 4 * own_rows].reshape(2, 2, own_rows, features)
    kept = lax.dynamic_index_in_dim(rows, z_hi, 1, keepdims=False)
    sent = lax.dynamic_index_in_dim(rows, 1 - z_hi, 1, keepdims=False).astype(BF16)
    gain_sum = totals[4 * own_rows] + totals[4 * own_rows + 1]
    gain_high = lax.reduce_precision(gain_sum, 8, 7)
    gain_sent = jnp.stack([gain_high, gain_sum - gain_high]).astype(BF16)
    sent = jnp.concatenate([sent.reshape(2 * own_rows, features), gain_sent])
    got = lax.ppermute(sent, "tensor", ZFAR).astype(F32)
    rows = kept + got[: 2 * own_rows].reshape(kept.shape)
    mlp_out = rows[0].astype(BF16)
    d_normed = rows[1]
    gain_sent = gain_sent.astype(F32)
    grad_gain = ((gain_sent[0] + gain_sent[1]) + (got[-2] + got[-1])) * root
    scaled = d_normed * norm_gain
    grad_tokens = (
        inverse_rms * (scaled - unit_rows * jnp.mean(scaled * unit_rows, axis=-1, keepdims=True))
    ).astype(BF16)
    grad_gate_up = join(gate_kept, gate_got, up_kept, up_got)
    return (
        mlp_out,
        grad_tokens,
        grad_gate_up,
        grad_down,
        grad_gain,
        peak[:1],
        peak[64:65],
    )


def solution(mesh):
    placed = (
        P(("dp", "tensor"), None),
        P(None, None, "tensor"),
        P("tensor", None),
        P(),
        P(),
        P(),
        P(("dp", "tensor"), None),
    )
    return jax.shard_map(
        shards,
        mesh=mesh,
        in_specs=placed,
        out_specs=(
            P(("dp", "tensor"), None),
            P(("dp", "tensor"), None),
            P("dp", None, "tensor"),
            P(("tensor", "dp"), None),
            P(),
            P(),
            P(),
        ),
        check_vma=False,
    )
```

```python
import functools
import math

import jax
import jax.numpy as jnp
from jax import lax
from jax.experimental import pallas as pl
from jax.experimental.pallas import tpu as pltpu
from jax.sharding import PartitionSpec as P

PEAK = 448.0
EPSILON = 1e-05
ROWS = (((0,), (0,)), ((), ()))
COLS = (((1,), (1,)), ((), ()))
F32 = jnp.float32
BF16 = jnp.bfloat16
MIB = 1024 * 1024
SMEM = pltpu.SMEM
VMEM = pltpu.VMEM


def options(mib):
    return pltpu.CompilerParams(
        dimension_semantics=("arbitrary",), vmem_limit_bytes=mib * MIB
    )


def cost(macs, moved):
    return pl.CostEstimate(flops=2 * macs, bytes_accessed=moved, transcendentals=0)


def forward_kernel(
    steps, act_ref, own_ref, other_ref, gain_ref, wg_ref, wu_ref,
    hidden_ref, slope_ref, silu_ref, inverse_ref, peak_ref, q_ref, gate_ref, up_ref,
):
    step = pl.program_id(0)
    group = own_ref.shape[1]
    half = own_ref.shape[0] * group
    depth = wg_ref.shape[0]
    chunk = 2 * group

    def take(source, r, columns):
        block = source[r // group : r // group + 2, :, columns]
        return block.reshape(chunk, block.shape[2])

    def quantized(k, slot):
        scale = PEAK / act_ref[0]
        columns = pl.ds(pl.multiple_of(k * depth, depth), depth)
        gain = gain_ref[:, columns]
        peak = peak_ref[...]
        for source, base in ((own_ref, 0), (other_ref, half)):
            for r in range(0, half, chunk):
                rows = pl.ds(base + r, chunk)
                values = take(source, r, columns).astype(F32)
                normed = (values * inverse_ref[rows, :1]) * gain
                q_ref[slot, rows, :] = jnp.clip(normed * scale, -PEAK, PEAK).astype(BF16)
                size = jnp.abs(normed)
                for c in range(0, depth, 128):
                    peak = jnp.maximum(peak, size[:, c : c + 128])
        peak_ref[...] = peak

    @pl.when(step == 0)
    def _():
        peak_ref[...] = jnp.zeros_like(peak_ref)
        gate_ref[...] = jnp.zeros_like(gate_ref)
        up_ref[...] = jnp.zeros_like(up_ref)
        features = own_ref.shape[2]
        for source, base in ((own_ref, 0), (other_ref, half)):
            for r in range(0, half, chunk):
                total = jnp.zeros((chunk, 128), F32)
                for c in range(0, features, 128):
                    values = take(source, r, pl.ds(c, 128)).astype(F32)
                    total += values * values
                mean = jnp.sum(total, axis=-1, keepdims=True) / features
                inverse_ref[pl.ds(base + r, chunk), :] = jnp.broadcast_to(
                    lax.rsqrt(mean + EPSILON), (chunk, 128)
                )
        quantized(0, 0)

    slot = lax.rem(step, 2)
    block = q_ref[slot]
    gate_ref[...] += jnp.dot(block, wg_ref[...], preferred_element_type=F32)
    up_ref[...] += jnp.dot(block, wu_ref[...], preferred_element_type=F32)

    @pl.when(step < steps - 1)
    def _():
        quantized(step + 1, 1 - slot)

    @pl.when(step == steps - 1)
    def _():
        unit = act_ref[0] / PEAK

        @pl.loop(0, gate_ref.shape[0], step=32)
        def _(r):
            rows = pl.ds(pl.multiple_of(r, 32), 32)
            pre_gate = gate_ref[rows, :] * unit
            pre_up = up_ref[rows, :] * unit
            sigmoid = jax.nn.sigmoid(pre_gate)
            silu = pre_gate * sigmoid
            hidden_ref[rows, :] = (silu * pre_up).astype(BF16)
            silu_ref[rows, :] = silu
            slope_ref[rows, :] = pre_up * sigmoid * (1.0 + pre_gate * (1.0 - sigmoid))


def forward(act_history, own, other, gain, paired, depth=1024):
    half, features = own.shape[0] * own.shape[2], own.shape[3]
    width = paired.shape[1] // 2
    steps = features // depth
    rows = 2 * half
    whole = lambda *shape: pl.BlockSpec(shape, lambda i: (0,) * len(shape))
    token_rows = pl.BlockSpec((8, None, own.shape[2], features), lambda i: (0, 0, 0, 0))
    return pl.pallas_call(
        functools.partial(forward_kernel, steps),
        grid=(steps,),
        in_specs=[
            pl.BlockSpec(memory_space=SMEM),
            token_rows,
            token_rows,
            whole(1, features),
            pl.BlockSpec((depth, width), lambda i: (i, 0)),
            pl.BlockSpec((depth, width), lambda i: (i, 1)),
        ],
        out_specs=[
            whole(rows, width),
            whole(rows, width),
            whole(rows, width),
            whole(rows, 128),
            whole(32, 128),
        ],
        out_shape=[
            jax.ShapeDtypeStruct((rows, width), BF16),
            jax.ShapeDtypeStruct((rows, width), F32),
            jax.ShapeDtypeStruct((rows, width), F32),
            jax.ShapeDtypeStruct((rows, 128), F32),
            jax.ShapeDtypeStruct((32, 128), F32),
        ],
        scratch_shapes=[
            VMEM((2, rows, depth), BF16),
            VMEM((rows, width), F32),
            VMEM((rows, width), F32),
        ],
        compiler_params=options(62),
        cost_estimate=cost(rows * features * width * 2, paired.size * 2),
        name="forward",
    )(act_history, own, other, gain, paired, paired)


def both_rows(own_ref, other_ref):
    groups, rows, depth = own_ref.shape
    own = own_ref[...].reshape(groups * rows, depth)
    return jnp.concatenate([own, other_ref[...].reshape(groups * rows, depth)])


def backward_kernel(
    steps, history_ref, own_ref, other_ref, down_ref, slope_ref, silu_ref,
    gate_ref, up_ref, peak_ref, total_ref,
):
    step = pl.program_id(0)

    @pl.when(step == 0)
    def _():
        total_ref[...] = jnp.zeros_like(total_ref)
        peak_ref[...] = jnp.zeros_like(peak_ref)

    values = both_rows(own_ref, other_ref).astype(F32)
    peak_ref[...] = jnp.maximum(peak_ref[...], jnp.max(jnp.abs(values)))
    block = jnp.clip(values * (PEAK / history_ref[0]), -PEAK, PEAK).astype(BF16)
    total_ref[...] += lax.dot_general(block, down_ref[...], COLS, preferred_element_type=F32)

    @pl.when(step == steps - 1)
    def _():
        d_hidden = total_ref[...] * (history_ref[0] / PEAK)
        gate_ref[...] = (d_hidden * slope_ref[...]).astype(BF16)
        up_ref[...] = (d_hidden * silu_ref[...]).astype(BF16)


def backward(grad_history, own, other, down, slope, silu, depth=1024):
    half, features = own.shape[0] * own.shape[2], own.shape[3]
    strip = pl.BlockSpec((8, None, own.shape[2], depth), lambda i: (0, 1, 0, i))
    width = down.shape[0]
    steps = features // depth
    rows = 2 * half
    whole = lambda *shape: pl.BlockSpec(shape, lambda i: (0,) * len(shape))
    return pl.pallas_call(
        functools.partial(backward_kernel, steps),
        grid=(steps,),
        in_specs=[
            pl.BlockSpec(memory_space=SMEM),
            strip,
            strip,
            pl.BlockSpec((width, depth), lambda i: (0, i)),
            whole(rows, width),
            whole(rows, width),
        ],
        out_specs=[whole(rows, width), whole(rows, width), whole(8, 128)],
        out_shape=[
            jax.ShapeDtypeStruct((rows, width), BF16),
            jax.ShapeDtypeStruct((rows, width), BF16),
            jax.ShapeDtypeStruct((8, 128), F32),
        ],
        scratch_shapes=[VMEM((rows, width), F32)],
        compiler_params=options(62),
        cost_estimate=cost(rows * features * width, down.size * 2),
        name="backward",
    )(grad_history, own, other, down, slope, silu)


def out_kernel(hidden_ref, down_ref, own_ref, other_ref):
    half = own_ref.shape[0]
    share = jnp.dot(hidden_ref[...], down_ref[...], preferred_element_type=F32).astype(BF16)
    own_ref[...] = share[:half]
    other_ref[...] = share[half:]


def out_shares(hidden, down, depth=1024):
    rows, width = hidden.shape
    half, features = rows // 2, down.shape[1]
    strip = pl.BlockSpec((half, depth), lambda i: (0, i))
    return pl.pallas_call(
        out_kernel,
        grid=(features // depth,),
        in_specs=[
            pl.BlockSpec((rows, width), lambda i: (0, 0)),
            pl.BlockSpec((width, depth), lambda i: (0, i)),
        ],
        out_specs=[strip, strip],
        out_shape=[jax.ShapeDtypeStruct((half, features), BF16)] * 2,
        compiler_params=options(62),
        cost_estimate=cost(rows * features * width // 50, down.size // 25),
        name="out_shares",
    )(hidden, down)


def normed_kernel(
    gate_ref, up_ref, wg_ref, wu_ref, own_ref, other_ref, inverse_ref,
    norm_own_ref, norm_other_ref, gain_ref,
):
    half = norm_own_ref.shape[0]
    normed = lax.dot_general(gate_ref[...], wg_ref[...], COLS, preferred_element_type=F32)
    normed += lax.dot_general(up_ref[...], wu_ref[...], COLS, preferred_element_type=F32)
    norm_own_ref[...] = normed[:half].astype(BF16)
    norm_other_ref[...] = normed[half:].astype(BF16)
    unit = both_rows(own_ref, other_ref).astype(F32) * inverse_ref[:, :1]
    gain_ref[...] = jnp.sum(normed * unit, axis=0, keepdims=True)


def normed_shares(d_gate, d_up, paired, own, other, inverse, depth=1024):
    half, features = own.shape[0] * own.shape[2], own.shape[3]
    rows, width = d_gate.shape
    token_rows = pl.BlockSpec((8, None, own.shape[2], depth), lambda i: (0, 0, 0, i))
    whole = lambda *shape: pl.BlockSpec(shape, lambda i: (0,) * len(shape))
    strip = pl.BlockSpec((half, depth), lambda i: (0, i))
    return pl.pallas_call(
        normed_kernel,
        grid=(features // depth,),
        in_specs=[
            whole(rows, width),
            whole(rows, width),
            pl.BlockSpec((depth, width), lambda i: (i, 0)),
            pl.BlockSpec((depth, width), lambda i: (i, 1)),
            token_rows,
            token_rows,
            whole(rows, 128),
        ],
        out_specs=[strip, strip, pl.BlockSpec((1, depth), lambda i: (0, i))],
        out_shape=[jax.ShapeDtypeStruct((half, features), BF16)] * 2
        + [jax.ShapeDtypeStruct((1, features), F32)],
        compiler_params=options(62),
        cost_estimate=cost(rows * features * width * 2, paired.size * 2),
        name="normed_shares",
    )(d_gate, d_up, paired, paired, own, other, inverse)


def pack_kernel(out_own, out_got, norm_own, norm_got, gain_ref, parts_ref):
    across = parts_ref.shape[0]
    rows = out_own.shape[0] // (2 * across)
    place = 0
    for own, got in ((out_own, out_got), (norm_own, norm_got)):
        total = (own[...].astype(F32) + got[...].astype(F32)).astype(BF16)
        for h in range(2):
            for y in range(across):
                base = (h * across + y) * rows
                parts_ref[y, place : place + rows] = total[base : base + rows]
            place += rows
    gain = gain_ref[...]
    upper = gain.astype(BF16)
    lower = (gain - upper.astype(F32)).astype(BF16)
    both = jnp.concatenate([upper, lower])
    for y in range(across):
        parts_ref[y, place:] = both


def pack(out_own, out_got, norm_own, norm_got, gain, rows, depth=1024):
    half, features = out_own.shape
    strip = pl.BlockSpec((half, depth), lambda i: (0, i))
    total = 4 * rows + 2
    return pl.pallas_call(
        pack_kernel,
        grid=(features // depth,),
        in_specs=[strip] * 4 + [pl.BlockSpec((1, depth), lambda i: (0, i))],
        out_specs=pl.BlockSpec((4, total, depth), lambda i: (0, 0, i)),
        out_shape=jax.ShapeDtypeStruct((4, total, features), BF16),
        compiler_params=options(62),
        cost_estimate=cost(half * features // 25, half * features // 4),
        name="pack",
    )(out_own, out_got, norm_own, norm_got, gain)


def slice_block(own_ref, other_ref):
    parts = []
    for ring in range(4):
        for source in (own_ref, other_ref):
            block = source[:, ring]
            parts.append(block.reshape(block.shape[0] * block.shape[1], block.shape[2]))
    return jnp.concatenate(parts)


def stack_rows(pieces, all_ref):
    rows = pieces[0].shape[0]
    for ring, piece in enumerate(pieces):
        all_ref[ring * rows : (ring + 1) * rows, :] = piece[...]


def pair_kernel(at_ref, scale_ref, p0, p1, p2, p3, own_ref, other_ref, out_ref, all_ref):
    @pl.when(pl.program_id(0) == 0)
    def _():
        stack_rows((p0, p1, p2, p3), all_ref)

    block = slice_block(own_ref, other_ref)
    total = lax.dot_general(block, all_ref[...], ROWS, preferred_element_type=F32)
    out_ref[...] = (total * scale_ref[0]).astype(BF16)


def down_kernel(at_ref, scale_ref, p0, p1, p2, p3, own_ref, other_ref, out_ref, all_ref):
    @pl.when(pl.program_id(0) == 0)
    def _():
        stack_rows((p0, p1, p2, p3), all_ref)

    block = slice_block(own_ref, other_ref)
    total = lax.dot_general(all_ref[...], block, ROWS, preferred_element_type=F32)
    out_ref[...] = (total * scale_ref[0]).astype(BF16)


def contract(kernel, scale, pieces, own, other, kind, first, count, share=1, depth=256):
    rows, width = pieces[0].shape
    piece = pl.BlockSpec((rows, width), lambda i, at: (0, 0))
    steps = count // depth
    block = (own.shape[0], 4, None, own.shape[3], depth)
    cut = pl.BlockSpec(block, lambda i, at: (0, 0, kind, 0, at[0] * steps + i))
    if kernel is pair_kernel:
        shape, spec = (count, width), pl.BlockSpec((depth, width), lambda i, at: (i, 0))
    else:
        shape, spec = (width, count), pl.BlockSpec((width, depth), lambda i, at: (0, i))
    return pl.pallas_call(
        kernel,
        grid_spec=pltpu.PrefetchScalarGridSpec(
            num_scalar_prefetch=1,
            grid=(steps,),
            in_specs=[pl.BlockSpec(memory_space=SMEM)] + [piece] * 4 + [cut, cut],
            out_specs=spec,
            scratch_shapes=[VMEM((4 * rows, width), BF16)],
        ),
        out_shape=jax.ShapeDtypeStruct(shape, BF16),
        compiler_params=options(62),
        cost_estimate=cost(4 * rows * width * count // share, 8 * rows * (width + count) // share),
        name="contract_" + ("pair" if kernel is pair_kernel else "down"),
    )(first.reshape(1).astype(jnp.int32), scale, *pieces, own, other)


def add_kernel(kept_ref, got_ref, out_ref):
    total = kept_ref[...].astype(F32) + got_ref[...].astype(F32)
    out_ref[...] = total.astype(BF16)


def add(kept, got, depth=512):
    rows, columns = kept.shape
    strip = pl.BlockSpec((rows, depth), lambda i: (0, i))
    return pl.pallas_call(
        add_kernel,
        grid=(columns // depth,),
        in_specs=[strip, strip],
        out_specs=strip,
        out_shape=jax.ShapeDtypeStruct((rows, columns), BF16),
        compiler_params=options(62),
        cost_estimate=cost(rows * columns // 50, rows * columns // 8),
        name="add",
    )(kept, got)


def join_kernel(g0, g1, u0, u1, out_ref):
    out_ref[:, 0, :] = (g0[...].astype(F32) + g1[...].astype(F32)).astype(BF16)
    out_ref[:, 1, :] = (u0[...].astype(F32) + u1[...].astype(F32)).astype(BF16)


def join(gate_kept, gate_got, up_kept, up_got, depth=128):
    rows, width = gate_kept.shape
    strip = pl.BlockSpec((depth, width), lambda i: (i, 0))
    return pl.pallas_call(
        join_kernel,
        grid=(rows // depth,),
        in_specs=[strip] * 4,
        out_specs=pl.BlockSpec((depth, 2, width), lambda i: (i, 0, 0)),
        out_shape=jax.ShapeDtypeStruct((rows, 2, width), BF16),
        compiler_params=options(62),
        cost_estimate=cost(rows * width, rows * width * 12),
        name="join",
    )(gate_kept, gate_got, up_kept, up_got)

RINGS = [[2 * k + core for k in range(8)] for core in range(2)]
CORE = [(i, i ^ 1) for i in range(16)]
ZPAIR = [(i, i ^ 4) for i in range(8)]
LINES = [[8 * high + 2 * y + core for y in range(4)] for high in range(2) for core in range(2)]
ZFAR = [(i, i ^ 8) for i in range(16)]


def send_y(block, step):
    ring = [
        (8 * high + 2 * y + core, 8 * high + 2 * ((y + step) % 4) + core)
        for high in range(2)
        for y in range(4)
        for core in range(2)
    ]
    return lax.ppermute(block, "tensor", ring)


def exchange(parts):
    return lax.all_to_all(parts, "tensor", 0, 0, tiled=True, axis_index_groups=RINGS)


def exchange_y(parts):
    return lax.all_to_all(parts, "tensor", 0, 0, tiled=True, axis_index_groups=LINES)


def gather_ring(block):
    return exchange(jnp.broadcast_to(block[None], (8,) + block.shape))


def swap_core(block):
    return lax.ppermute(block, "tensor", CORE)


def send_x(block, step):
    ring = [(z * 4 + x, z * 4 + (x + step) % 4) for z in range(2) for x in range(4)]
    return lax.ppermute(block, "dp", ring)


def quantize(values, unit):
    return jnp.clip(values * unit, -PEAK, PEAK).astype(BF16)


def together(*values):
    return lax.optimization_barrier(values)


def after(value, *others):
    return lax.optimization_barrier((value,) + others)[0]


def shards(tokens, gate_up, down_proj, norm_gain, act_history, grad_history, grad_out):
    own_rows, features = tokens.shape
    width = down_proj.shape[0]
    groups = lax.axis_size("dp")
    lanes = lax.axis_size("tensor")
    root = 1.0 / math.sqrt(own_rows * groups * lanes)
    pair_scale = act_history / PEAK * root
    down_scale = grad_history / PEAK * root
    dp = lax.axis_index("dp")
    z_lo = dp // 4
    x = dp % 4
    z_hi = lax.axis_index("tensor") // 8
    span = features // 8
    half = own_rows * 8

    rows_own = gather_ring(jnp.stack([tokens, grad_out]))
    paired = gate_up.reshape(features, 2 * width)

    values = after(tokens, paired).astype(F32)
    inverse_rms = lax.rsqrt(jnp.mean(values * values, axis=-1, keepdims=True) + EPSILON)
    unit_rows = values * inverse_rms
    q_mine = quantize(unit_rows * norm_gain, PEAK / act_history[0])
    g_mine = quantize(grad_out.astype(F32), PEAK / grad_history[0])

    both = jnp.stack([q_mine, g_mine]).reshape(2 * own_rows, 2, 4, span)

    def columns(step):
        cut = lax.dynamic_slice(both, (0, 0, (x + step) % 4, 0), (2 * own_rows, 2, 1, span))
        return cut.reshape(2 * own_rows, 2 * span)

    sliced = jnp.stack(
        [columns(0), send_x(columns(1), 1), send_x(columns(-1), -1), send_x(columns(2), 2)]
    )
    rows_own = after(rows_own, sliced)
    rows_other = swap_core(rows_own)

    hidden, slope, silu, inverse, act_peak = forward(
        act_history, rows_own, rows_other, norm_gain.reshape(1, features), paired
    )
    hidden, sliced = together(hidden, sliced)

    slices_own = gather_ring(sliced.reshape(8 * own_rows, 2 * span))
    hidden_left, hidden_right = send_x(hidden, 1), send_x(hidden, -1)
    d_gate, d_up, grad_peak = backward(grad_history, rows_own, rows_other, down_proj, slope, silu)
    hidden, hidden_left, hidden_right, d_gate, d_up = together(
        hidden, hidden_left, hidden_right, d_gate, d_up
    )

    hidden_far = send_x(hidden, 2)
    gate_left, gate_right = send_x(d_gate, 1), send_x(d_gate, -1)
    norm_own, norm_other, gain_share = normed_shares(
        d_gate, d_up, paired, rows_own, rows_other, inverse
    )
    out_own, out_other = out_shares(after(hidden, norm_own), down_proj)
    gain_share = gain_share + swap_core(gain_share)
    peaks = jnp.concatenate(
        [jnp.full((1, 64), jnp.max(act_peak)), jnp.full((1, 64), jnp.max(grad_peak))], axis=1
    )
    small = jnp.concatenate([gain_share.reshape(-1, 128), peaks])
    small = jnp.broadcast_to(small[None], (groups,) + small.shape)
    hidden, hidden_far, gate_left, gate_right, norm_own, norm_other, small, d_gate, d_up = together(
        hidden, hidden_far, gate_left, gate_right, norm_own, norm_other, small, d_gate, d_up
    )
    slices_own, norm_other, out_own, out_other = together(
        slices_own, norm_other, out_own, out_other
    )
    slices_own = slices_own.reshape(8, 4, 2, own_rows, 2 * span)
    slices_other = swap_core(slices_own)
    hidden_all = (hidden, hidden_left, hidden_right, hidden_far)

    norm_got = swap_core(norm_other)
    out_got = swap_core(out_other)
    small = lax.all_to_all(small, "dp", 0, 0, tiled=True)
    gate_far = send_x(d_gate, 2)
    down_part = contract(
        down_kernel, down_scale, hidden_all, slices_own, slices_other, 1, z_lo * 0, 2 * span
    )
    hand = width // 2
    sent_down = lax.dynamic_slice(down_part, ((1 - z_lo) * hand, 0), (hand, 2 * span))
    kept_down = lax.dynamic_slice(down_part, (z_lo * hand, 0), (hand, 2 * span))
    sent_down, gate_far, norm_got, out_got, small, d_up = together(
        sent_down, gate_far, norm_got, out_got, small, d_up
    )
    gate_all = (d_gate, gate_left, gate_right, gate_far)

    def pair_part(pieces, place, share=1, scale=pair_scale):
        return contract(
            pair_kernel, scale, pieces, slices_own, slices_other, 0, place, span, share
        )

    got_down = lax.ppermute(sent_down, "dp", ZPAIR)
    up_all = (d_up, send_x(d_up, 1), send_x(d_up, -1), send_x(d_up, 2))
    gate_sent = pair_part(gate_all, 1 - z_lo)
    gain_sum = jnp.sum(small[:, :-1], axis=0).reshape(1, features)
    peak = jnp.max(small[:, -1], axis=0)
    parts = pack(out_own, out_got, norm_own, norm_got, after(gain_sum, gate_sent), own_rows)
    sums = exchange_y(parts)
    got_down, up_all, gate_sent, parts, late_scale = together(
        got_down, up_all, gate_sent, parts, pair_scale
    )

    gate_got = lax.ppermute(gate_sent, "dp", ZPAIR)
    up_sent = pair_part(up_all, 1 - z_lo, 50, late_scale)
    up_got = lax.ppermute(up_sent, "dp", ZPAIR)
    gate_kept = pair_part(gate_all, z_lo, 50, after(late_scale, up_sent))
    sum_down = add(kept_down, after(got_down, gate_kept))
    gate_got, gate_kept, sum_down, late_scale = together(
        gate_got, gate_kept, sum_down, late_scale
    )

    sum_down = sum_down.reshape(4, hand // 4, 2 * span)

    def own_part(step):
        return lax.dynamic_index_in_dim(sum_down, (x + step) % 4, 0, keepdims=False)

    turned = jnp.stack(
        [own_part(0), send_x(own_part(1), 1), send_x(own_part(2), 2), send_x(own_part(-1), -1)]
    )
    up_kept = pair_part(up_all, z_lo, scale=after(late_scale, sum_down))
    turned, up_kept = together(turned, up_kept)
    turned = turned[(x - jnp.arange(4)) % 4]
    grad_down = (
        turned.reshape(4, hand // 4, 2, span).transpose(1, 2, 0, 3).reshape(hand // 4, features)
    )

    gate_got, up_got, gate_kept, up_kept, grad_down, sums = together(
        gate_got, up_got, gate_kept, up_kept, grad_down, sums
    )
    totals = jnp.sum(sums.astype(F32), axis=0)
    rows = totals[: 4 * own_rows].reshape(2, 2, own_rows, features)
    kept = lax.dynamic_index_in_dim(rows, z_hi, 1, keepdims=False)
    sent = lax.dynamic_index_in_dim(rows, 1 - z_hi, 1, keepdims=False).astype(BF16)
    gain_sum = totals[4 * own_rows] + totals[4 * own_rows + 1]
    gain_high = lax.reduce_precision(gain_sum, 8, 7)
    gain_sent = jnp.stack([gain_high, gain_sum - gain_high]).astype(BF16)
    sent = jnp.concatenate([sent.reshape(2 * own_rows, features), gain_sent])
    got = lax.ppermute(sent, "tensor", ZFAR).astype(F32)
    rows = kept + got[: 2 * own_rows].reshape(kept.shape)
    mlp_out = rows[0].astype(BF16)
    d_normed = rows[1]
    gain_sent = gain_sent.astype(F32)
    grad_gain = ((gain_sent[0] + gain_sent[1]) + (got[-2] + got[-1])) * root
    scaled = d_normed * norm_gain
    grad_tokens = (
        inverse_rms * (scaled - unit_rows * jnp.mean(scaled * unit_rows, axis=-1, keepdims=True))
    ).astype(BF16)
    grad_gate_up = join(gate_kept, gate_got, up_kept, up_got)
    return (
        mlp_out,
        grad_tokens,
        grad_gate_up,
        grad_down,
        grad_gain,
        peak[:1],
        peak[64:65],
    )


def solution(mesh):
    placed = (
        P(("dp", "tensor"), None),
        P(None, None, "tensor"),
        P("tensor", None),
        P(),
        P(),
        P(),
        P(("dp", "tensor"), None),
    )
    return jax.shard_map(
        shards,
        mesh=mesh,
        in_specs=placed,
        out_specs=(
            P(("dp", "tensor"), None),
            P(("dp", "tensor"), None),
            P("dp", None, "tensor"),
            P(("tensor", "dp"), None),
            P(),
            P(),
            P(),
        ),
        check_vma=False,
    )
```
